32 devices in a mesh: dp: 8 (over z, y), tensor: 4 (over x, core).
Axes of the slice: x: 2, y: 2, z: 4, core: 2. Of those that a mesh axis runs over, the one named last changes fastest.
Arguments:
- d_out: bfloat16 [4096, 2560], P(('dp', 'tensor')), may hold values from -2.5 to 2.5
- gate_pre: bfloat16 [4096, 7168], P('dp', 'tensor'), may hold values from -6 to 6
- up_pre: bfloat16 [4096, 7168], P('dp', 'tensor'), may hold values from -40 to 40
- w_down: float32 [2560, 7168], P('dp', 'tensor'), may hold values from -280 to 280
- momentum: float32 [2560, 7168], P('dp', 'tensor'), may hold values from -3 to 3
Outputs:
- d_gate: bfloat16 [4096, 7168], P('dp', 'tensor')
- d_up: bfloat16 [4096, 7168], P('dp', 'tensor')
- w_new: float32 [2560, 7168], P('dp', 'tensor')
- momentum_new: float32 [2560, 7168], P('dp', 'tensor')
The draws below stay inside these ranges and needn't reach their ends.
All inputs are finite; a program needn't handle non-finite values.
Results may differ from the reference program's by a relative error of at most 0.0049.
Values may be sent and summed in bfloat16 or wider, within the bound.
No kernel may reach another device: no remote copies, remote signals or barrier semaphores. Data moves between devices by JAX's collectives and lax.ppermute only.
A program may use at most 128 MiB of HBM per device.

```python
import jax
import jax.numpy as jnp
from jax import lax

D = 2560
FF = 7168
TOKENS = 4096


def spread_factors(key, number):
    return jnp.exp(jax.random.uniform(key, (number,), jnp.float32, -1.1513, 1.1513))


def draw_d_out(key, part):
    key = jax.random.fold_in(key, 11)
    key_base, key_cols = jax.random.split(key)
    base = jnp.clip(jax.random.normal(key_base, (TOKENS, D), jnp.float32), -4.0, 4.0)
    values = 0.18 * base * spread_factors(key_cols, D)[None, :]
    return values.astype(jnp.bfloat16)


def draw_up_pre(key, part):
    key = jax.random.fold_in(key, 23)
    key_base, key_cols = jax.random.split(key)
    base = jnp.clip(jax.random.normal(key_base, (TOKENS, FF), jnp.float32), -4.0, 4.0)
    ramp = 1.0 + 2.0 * jnp.arange(FF, dtype=jnp.float32) / (FF - 1)
    values = base * (spread_factors(key_cols, FF) * ramp)[None, :]
    return values.astype(jnp.bfloat16)


def draw_w_down(key, part):
    key = jax.random.fold_in(key, 37)
    key_base, key_rows, key_cols = jax.random.split(key, 3)
    base = jnp.clip(jax.random.normal(key_base, (D, FF), jnp.float32), -4.0, 4.0)
    ramp = 1.0 + 2.0 * jnp.arange(FF, dtype=jnp.float32) / (FF - 1)
    column_scale = spread_factors(key_cols, FF) * ramp
    row_scale = spread_factors(key_rows, D)
    return (2.3 * base * row_scale[:, None] * column_scale[None, :]).astype(jnp.float32)


def block_scale(rng, dims, pieces, least, high):
    def one(dim, shards_of):
        draws = jax.random.uniform(jax.random.fold_in(jax.random.fold_in(rng, 6), dim), (shards_of,), jnp.float32, least / len(pieces), high / len(pieces))
        return jnp.repeat(jnp.exp(draws), dims[dim] // shards_of).reshape((-1,) + (1,) * (len(dims) - dim - 1))

    level = one(*pieces[0])
    for cut in pieces[1:]:
        level = level * one(*cut)
    return level


def normal_values(stream_key, shape, scale, limit, cuts=(), kind=jnp.bfloat16):
    values = scale * jax.random.normal(stream_key, shape, jnp.float32)
    if cuts:
        values = values * block_scale(stream_key, shape, cuts, -0.22, 0.18)
    return jnp.clip(values, -limit, limit).astype(kind)


def setup_inputs(seed: int = 0) -> dict:
    seeds = jax.random.split(jax.random.key(seed), 6)
    return {
        "d_out": draw_d_out(jax.random.fold_in(seeds[5], 71), 0),
        "gate_pre": normal_values(seeds[1], (TOKENS, FF), 1.0, 6.0, ((0, 8), (1, 4))),
        "up_pre": draw_up_pre(jax.random.fold_in(seeds[5], 71), 0),
        "w_down": draw_w_down(jax.random.fold_in(seeds[5], 71), 0),
        "momentum": normal_values(seeds[4], (D, FF), 0.5, 3.0, ((0, 8), (1, 4)), jnp.float32),
    }


def reference(d_out, gate_pre, up_pre, w_down, momentum):
    multiplier = FF ** (-0.5)
    gate_value = gate_pre.astype(jnp.float32)
    up_value = up_pre.astype(jnp.float32)
    sigmoid_gate = jax.nn.sigmoid(gate_value)
    hidden = (gate_value * sigmoid_gate * up_value).astype(jnp.bfloat16)
    w_low = w_down.astype(jnp.bfloat16)
    d_hidden = jnp.dot(d_out, w_low, preferred_element_type=jnp.float32) * multiplier
    d_gate = (d_hidden * up_value * sigmoid_gate * (1.0 + gate_value * (1.0 - sigmoid_gate))).astype(jnp.bfloat16)
    d_up = (d_hidden * gate_value * sigmoid_gate).astype(jnp.bfloat16)
    grad = jnp.dot(d_out.T, hidden, preferred_element_type=jnp.float32) * multiplier
    w_norm = jnp.sqrt(lax.optimization_barrier(jnp.sum(w_down * w_down, axis=1, keepdims=True)))
    g_norm = jnp.sqrt(lax.optimization_barrier(jnp.sum(grad * grad, axis=1, keepdims=True)) + 1e-06)
    factor = jnp.minimum(1.0, 0.1 * w_norm / g_norm)
    momentum_new = 0.9 * momentum + grad * factor
    w_new = w_down - 0.05 * momentum_new
    return (d_gate, d_up, w_new, momentum_new)
```

```python
import jax
import jax.numpy as jnp
from jax import lax
from jax.sharding import Mesh, PartitionSpec as P

FF = 7168
SWAP = [(0, 1), (1, 0)]
ORDER = {
    "own w": ["give w"],
    "over x": ["give w"],
    "hidden": ["own w"],
    "own half 1": ["give w"],
    "give a": ["over y 1", "shard"],
    "own half 2": ["hidden over y a"],
    "give b": ["over y 2", "partial 1a"],
    "gather 2E": ["send 1Ea"],
    "gather 2O": ["send 1Ea"],
    "mine b": ["gather 2E"],
    "send 1Eb": ["send 2Oa"],
    "send 2Ea": ["send 1Ea"],
    "send 2Oa": ["send 2Ea"],
    "gather 3E": ["send 1Eb"],
    "send 2Eb": ["gather 3E", "w squares"],
    "send 2Ob": ["send 2Eb"],
    "send 3Ea": ["send 2Ob"],
    "send 3Oa": ["send 3Ea"],
    "send 3Eb": ["back", "send 3Oa"],
    "send 3Ob": ["send 3Eb"],
    "grad a": ["send 3Ob"],
    "grad b": ["outputs"],
    "w squares": ["hidden over y a"],
    "diagonal 2": ["partial 1a"],
    "other 2": ["partial 1a"],
    "diagonal 1": ["shard"],
    "other 1": ["shard"],
}


def plane_sum(value):
    k = lax.axis_size("x") * 2
    across = [(i, k - 1 - i) for i in range(k)]
    return (
        value
        + lax.ppermute(value, "x", SWAP)
        + lax.ppermute(value, "c", SWAP)
        + lax.ppermute(value, ("x", "c"), across)
    )


def edges(n, parity, upward, downward):
    pairs = [(i, i + 1) for i in upward if i % 2 == parity]
    return pairs + [(i, i - 1) for i in downward if (i - 1) % 2 == parity]


class Graph:
    def __init__(self):
        self.rules, self.values, self.open = {}, {}, set()

    def rule(self, name, operand, work):
        self.rules[name] = (operand, work)

    def __getitem__(self, name):
        if name in self.values:
            return self.values[name]
        if name in self.open:
            raise ValueError("cycle at " + name)
        self.open.add(name)
        operand, work = self.rules[name]
        first = operand()
        waits = [self[other] for other in ORDER.get(name, ()) if other in self.rules]
        if waits:
            first = lax.optimization_barrier((first, waits))[0]
        self.values[name] = work(first)
        return self.values[name]


def body(d_out, gate_pre, up_pre, w_down, momentum):
    multiplier = FF ** (-0.5)
    n = lax.axis_size("z")
    z, y, x, c = (lax.axis_index(a) for a in ("z", "y", "x", "c"))
    rows = w_down.shape[0]
    height = 2 * rows
    cols = w_down.shape[1] // 2
    first = -(-cols // 256) * 128
    parts = {"a": (0, first), "b": (first, cols - first)}
    block, depth = d_out.shape
    half = n // 2 * height
    near_start = jnp.where(z < n // 2, depth - half, 0)
    starts = {"1": near_start, "2": depth - half - near_start}
    g = Graph()

    def in_order(a, b, axis):
        return jnp.where(
            y == 0, jnp.concatenate([a, b], axis=axis), jnp.concatenate([b, a], axis=axis)
        )

    def columns(a, start, width):
        return lax.dynamic_slice_in_dim(a, start, width, 1)

    def over(axis):
        return lambda value: lax.ppermute(value, axis, SWAP)

    def same(value):
        return value

    def weights(whose):
        return lambda w: columns(w, whose * cols, cols).astype(jnp.bfloat16)

    g.rule("give w", lambda: w_down, weights(1 - y))
    g.rule("own w", lambda: w_down, weights(y))
    g.rule("partner w", lambda: g["give w"], over("y"))
    g.rule("shard", lambda: in_order(g["own w"], g["partner w"], 0), same)
    g.rule("w squares", lambda: w_down, lambda w: jnp.sum(w * w, axis=1))

    def gather_pairs(s, parity):
        return edges(n, parity, range(s - 1, n - 1), range(1, n - s + 1))

    def gather(s, parity):
        pairs = gather_pairs(s, parity)
        if not pairs:
            return
        name, other = f"gather {s}{'EO'[parity]}", f"got {s - 1}{'OE'[parity]}"
        g.rule(name, (lambda: g["shard"]) if s == 1 else (lambda: g[other]), same)
        got = f"got {s}{'EO'[parity]}"
        g.rule(got, lambda: g[name], lambda v: lax.ppermute(v, "z", pairs))

    for s in range(1, n):
        gather(s, 0)
        gather(s, 1)

    def hidden(operands):
        gate, up = (v.astype(jnp.float32) for v in operands)
        return (gate * jax.nn.sigmoid(gate) * up).astype(jnp.bfloat16)

    g.rule("hidden", lambda: (gate_pre, up_pre), hidden)

    def hidden_part(p):
        start, width = parts[p]
        g.rule("mine " + p, lambda: columns(g["hidden"], y * cols + start, width), same)
        g.rule("give " + p, lambda: columns(g["hidden"], (1 - y) * cols + start, width), same)
        g.rule("hidden over y " + p, lambda: g["give " + p], over("y"))

    hidden_part("a")
    hidden_part("b")

    def arrange(operands):
        pair = jnp.concatenate(operands, axis=0)
        other = lax.ppermute(pair, "c", SWAP)
        out = jnp.zeros((4 * block, pair.shape[1]), pair.dtype)
        for source, core in ((pair, c), (other, 1 - c)):
            for k, chip in ((0, x), (1, 1 - x)):
                piece = source[k * block : (k + 1) * block]
                out = lax.dynamic_update_slice_in_dim(out, piece, (chip * 2 + core) * block, 0)
        return out

    g.rule("over x", lambda: d_out, over("x"))
    g.rule("group", lambda: (d_out, g["over x"]), arrange)

    def cotangents(k):
        g.rule("own half " + k, lambda: columns(d_out, starts[k], half), same)
        g.rule("over y " + k, lambda: g["own half " + k], over("y"))
        g.rule("diagonal " + k, lambda: g["over y " + k], over("x"))
        g.rule("other " + k, lambda: (g["over y " + k], g["diagonal " + k]), arrange)

    cotangents("1")
    cotangents("2")

    contract = (((0,), (0,)), ((), ()))

    def product(k, p):
        def work(mine):
            partial = lax.dot_general(
                columns(g["group"], starts[k], half),
                mine,
                contract,
                preferred_element_type=jnp.float32,
            ) + lax.dot_general(
                g["other " + k],
                g["hidden over y " + p],
                contract,
                preferred_element_type=jnp.float32,
            )
            return (partial * multiplier).astype(jnp.bfloat16)

        g.rule(f"partial {k}{p}", lambda: g["mine " + p], work)

    for k in starts:
        for p in parts:
            product(k, p)

    def chunk(p, k, s):
        k = jnp.clip(k, 0, n - 1) * height
        at = jnp.clip(k - starts["1"], 0, half - height)
        a = lax.dynamic_slice_in_dim(g["partial 1" + p], at, height, 0)
        if s <= n // 2:
            return a
        at = jnp.clip(k - starts["2"], 0, half - height)
        b = lax.dynamic_slice_in_dim(g["partial 2" + p], at, height, 0)
        return jnp.where((k >= starts["1"]) & (k < starts["1"] + half), a, b)

    def reduce(s, p, parity):
        pairs = edges(n, parity, range(0, s), range(n - s, n))
        if not pairs:
            return
        name, before = f"{s}{'EO'[parity]}{p}", f"{s - 1}{'OE'[parity]}{p}"

        def operand():
            value = chunk(p, jnp.where(z % 2 == parity, n - s + z, s - n + z), s)
            if "sum " + before not in g.rules:
                return value
            got = g["sum " + before]
            return (value.astype(jnp.float32) + got.astype(jnp.float32)).astype(value.dtype)

        g.rule("send " + name, operand, same)
        g.rule("sum " + name, lambda: g["send " + name], lambda v: lax.ppermute(v, "z", pairs))

    for s in range(1, n):
        for p in parts:
            reduce(s, p, 0)
            reduce(s, p, 1)

    def d_hidden_of(tokens):
        total = jnp.dot(
            columns(tokens, z * height, height), g["shard"], preferred_element_type=jnp.float32
        )
        for t in range(1, n):
            piece, place = g[f"got {t}E"], jnp.where(z % 2 == 0, z + t, z - t)
            if f"got {n - t}O" in g.rules:
                piece = jnp.where((place >= 0) & (place < n), piece, g[f"got {n - t}O"])
            total = total + jnp.dot(
                columns(tokens, place % n * height, height),
                piece,
                preferred_element_type=jnp.float32,
            )
        return (total * multiplier).astype(jnp.bfloat16)

    def other_tokens():
        a, b = g["other 1"], g["other 2"]
        return jnp.where(
            near_start == 0, jnp.concatenate([a, b], axis=1), jnp.concatenate([b, a], axis=1)
        )

    g.rule("back", other_tokens, d_hidden_of)
    g.rule("back over y", lambda: g["back"], over("y"))
    g.rule("here", lambda: g["group"], d_hidden_of)

    def gate_and_up(operands):
        gate, up = (v.astype(jnp.float32) for v in operands)
        d_hidden = in_order(g["here"], g["back over y"], 1).astype(jnp.float32)
        s = jax.nn.sigmoid(gate)
        d_gate = (d_hidden * up * s * (1.0 + gate * (1.0 - s))).astype(jnp.bfloat16)
        return d_gate, (d_hidden * gate * s).astype(jnp.bfloat16)

    g.rule("outputs", lambda: lax.optimization_barrier((gate_pre, up_pre, g["hidden"]))[:2], gate_and_up)

    def total(p):
        def work(even):
            whole = chunk(p, z, n).astype(jnp.float32) + even.astype(jnp.float32)
            return whole + g[f"sum {n - 1}O{p}"].astype(jnp.float32)

        g.rule("grad " + p, lambda: g[f"sum {n - 1}E{p}"], work)

        def rows_of(whose):
            low = g["grad " + p].astype(jnp.bfloat16)
            return lax.dynamic_slice_in_dim(low, whose * rows, rows, 0)

        g.rule("give grad " + p, lambda: rows_of(1 - y), same)
        g.rule("grad over y " + p, lambda: g["give grad " + p], over("y"))
        g.rule("keep grad " + p, lambda: rows_of(y), same)

    for p in parts:
        total(p)

    grad_square = sum(jnp.sum(g["grad " + p] * g["grad " + p], axis=1) for p in parts)
    keep = lax.dynamic_slice_in_dim(grad_square, y * rows, rows, 0)
    give = lax.dynamic_slice_in_dim(grad_square, (1 - y) * rows, rows, 0)
    grad_square = keep + lax.ppermute(give, "y", SWAP)
    squares = plane_sum(jnp.stack([g["w squares"], grad_square]))
    factor = jnp.minimum(1.0, 0.1 * jnp.sqrt(squares[0]) / jnp.sqrt(squares[1] + 1e-06))
    grad = in_order(
        jnp.concatenate([g["keep grad " + p] for p in parts], 1),
        jnp.concatenate([g["grad over y " + p] for p in parts], 1),
        1,
    ).astype(jnp.float32)
    momentum_new = 0.9 * momentum + grad * factor[:, None]
    w_new = w_down - 0.05 * momentum_new
    d_gate, d_up = g["outputs"]
    return (d_gate, d_up, w_new, momentum_new)


def solution(mesh):
    groups, parts = mesh.devices.shape
    fine = Mesh(mesh.devices.reshape(groups // 2, 2, parts // 2, 2), ("z", "y", "x", "c"))
    dp, tensor = ("z", "y"), ("x", "c")
    placed = P(dp, tensor)
    return jax.shard_map(
        body,
        mesh=fine,
        in_specs=(P(dp + tensor, None), placed, placed, placed, placed),
        out_specs=(placed,) * 4,
        check_vma=False,
    )
```

```python
import jax
import jax.numpy as jnp
from jax import lax
from jax.sharding import Mesh, PartitionSpec as P

FF = 7168
SWAP = [(0, 1), (1, 0)]
ORDER = {
    "ow": ["gw"],
    "x": ["gw"],
    "h": ["ow"],
    "d1": ["gw"],
    "sa": ["y1", "sh"],
    "d2": ["ta"],
    "sb": ["y2", "p1a"],
    "G2E": ["S1Ea"],
    "G2O": ["S1Ea"],
    "mb": ["G2E"],
    "S1Eb": ["S2Oa"],
    "S2Ea": ["S1Ea"],
    "S2Oa": ["S2Ea"],
    "G3E": ["S1Eb"],
    "S2Eb": ["G3E", "w2"],
    "S2Ob": ["S2Eb"],
    "S3Ea": ["S2Ob"],
    "S3Oa": ["S3Ea"],
    "S3Eb": ["b", "S3Oa"],
    "S3Ob": ["S3Eb"],
    "za": ["S3Ob"],
    "zb": ["out", "fa"],
    "w2": ["ta"],
    "q2": ["p1a"],
    "o2": ["p1a"],
    "q1": ["sh"],
    "o1": ["sh"],
}
EDGE = "EO"


def plane_sum(value):
    k = lax.axis_size("x") * 2
    across = [(i, k - 1 - i) for i in range(k)]
    return (
        value
        + lax.ppermute(value, "x", SWAP)
        + lax.ppermute(value, "c", SWAP)
        + lax.ppermute(value, ("x", "c"), across)
    )


def edges(n, parity, upward, downward):
    pairs = [(i, i + 1) for i in upward if i % 2 == parity]
    return pairs + [(i, i - 1) for i in downward if (i - 1) % 2 == parity]


class Graph:
    def __init__(self):
        self.rules, self.values, self.open = {}, {}, set()

    def rule(self, name, operand, work):
        self.rules[name] = (operand, work)

    def __getitem__(self, name):
        if name in self.values:
            return self.values[name]
        if name in self.open:
            raise ValueError(name)
        self.open.add(name)
        operand, work = self.rules[name]
        first = operand()
        waits = [self[other] for other in ORDER.get(name, ()) if other in self.rules]
        if waits:
            first = lax.optimization_barrier((first, waits))[0]
        self.values[name] = work(first)
        return self.values[name]


def body(d_out, gate_pre, up_pre, w_down, momentum):
    multiplier = FF ** (-0.5)
    n = lax.axis_size("z")
    z, y, x, c = (lax.axis_index(a) for a in ("z", "y", "x", "c"))
    rows = w_down.shape[0]
    height = 2 * rows
    cols = w_down.shape[1] // 2
    first = -(-cols // 256) * 128
    parts = {"a": (0, first), "b": (first, cols - first)}
    block, depth = d_out.shape
    half = n // 2 * height
    near_start = jnp.where(z < n // 2, depth - half, 0)
    starts = {"1": near_start, "2": depth - half - near_start}
    g = Graph()

    def in_order(a, b, axis):
        return jnp.where(
            y == 0, jnp.concatenate([a, b], axis=axis), jnp.concatenate([b, a], axis=axis)
        )

    def columns(a, start, width):
        return lax.dynamic_slice_in_dim(a, start, width, 1)

    def over(axis):
        return lambda value: lax.ppermute(value, axis, SWAP)

    def same(value):
        return value

    def weights(whose):
        return lambda w: columns(w, whose * cols, cols).astype(jnp.bfloat16)

    g.rule("gw", lambda: w_down, weights(1 - y))
    g.rule("ow", lambda: w_down, weights(y))
    g.rule("pw", lambda: g["gw"], over("y"))
    g.rule("sh", lambda: in_order(g["ow"], g["pw"], 0), same)
    g.rule("w2", lambda: w_down, lambda w: jnp.sum(w * w, axis=1))

    def gather_pairs(s, parity):
        return edges(n, parity, range(s - 1, n - 1), range(1, n - s + 1))

    def gather(s, parity):
        pairs = gather_pairs(s, parity)
        if not pairs:
            return
        name, got = [f"{kind}{s}{EDGE[parity]}" for kind in "GR"]
        other = f"R{s - 1}{EDGE[1 - parity]}"
        g.rule(name, (lambda: g["sh"]) if s == 1 else (lambda: g[other]), same)
        g.rule(got, lambda: g[name], lambda v: lax.ppermute(v, "z", pairs))

    for s in range(1, n):
        gather(s, 0)
        gather(s, 1)

    def hidden(operands):
        gate, up = (v.astype(jnp.float32) for v in operands)
        return (gate * jax.nn.sigmoid(gate) * up).astype(jnp.bfloat16)

    g.rule("h", lambda: (gate_pre, up_pre), hidden)

    def hidden_part(p):
        start, width = parts[p]
        g.rule("m" + p, lambda: columns(g["h"], y * cols + start, width), same)
        g.rule("s" + p, lambda: columns(g["h"], (1 - y) * cols + start, width), same)
        g.rule("t" + p, lambda: g["s" + p], over("y"))

    hidden_part("a")
    hidden_part("b")

    def arrange(operands):
        pair = jnp.concatenate(operands, axis=0)
        other = lax.ppermute(pair, "c", SWAP)
        out = jnp.zeros((4 * block, pair.shape[1]), pair.dtype)
        for source, core in ((pair, c), (other, 1 - c)):
            for k, chip in ((0, x), (1, 1 - x)):
                piece = source[k * block : (k + 1) * block]
                out = lax.dynamic_update_slice_in_dim(out, piece, (chip * 2 + core) * block, 0)
        return out

    g.rule("x", lambda: d_out, over("x"))
    g.rule("g", lambda: (d_out, g["x"]), arrange)

    def cotangents(k):
        g.rule("d" + k, lambda: columns(d_out, starts[k], half), same)
        g.rule("y" + k, lambda: g["d" + k], over("y"))
        g.rule("q" + k, lambda: g["y" + k], over("x"))
        g.rule("o" + k, lambda: (g["y" + k], g["q" + k]), arrange)

    cotangents("1")
    cotangents("2")

    contract = (((0,), (0,)), ((), ()))

    def product(k, p):
        def work(mine):
            partial = lax.dot_general(
                columns(g["g"], starts[k], half),
                mine,
                contract,
                preferred_element_type=jnp.float32,
            ) + lax.dot_general(
                g["o" + k],
                g["t" + p],
                contract,
                preferred_element_type=jnp.float32,
            )
            return (partial * multiplier).astype(jnp.bfloat16)

        g.rule("p" + k + p, lambda: g["m" + p], work)

    for k in starts:
        for p in parts:
            product(k, p)

    def chunk(p, k, s):
        k = jnp.clip(k, 0, n - 1) * height
        at = jnp.clip(k - starts["1"], 0, half - height)
        a = lax.dynamic_slice_in_dim(g["p1" + p], at, height, 0)
        if s <= n // 2:
            return a
        at = jnp.clip(k - starts["2"], 0, half - height)
        b = lax.dynamic_slice_in_dim(g["p2" + p], at, height, 0)
        return jnp.where((k >= starts["1"]) & (k < starts["1"] + half), a, b)

    def reduce(s, p, parity):
        pairs = edges(n, parity, range(0, s), range(n - s, n))
        if not pairs:
            return
        name, before = f"{s}{EDGE[parity]}{p}", f"T{s - 1}{EDGE[1 - parity]}{p}"

        def operand():
            value = chunk(p, jnp.where(z % 2 == parity, n - s + z, s - n + z), s)
            if before not in g.rules:
                return value
            got = g[before]
            return (value.astype(jnp.float32) + got.astype(jnp.float32)).astype(value.dtype)

        g.rule("S" + name, operand, same)
        g.rule("T" + name, lambda: g["S" + name], lambda v: lax.ppermute(v, "z", pairs))

    for s in range(1, n):
        for p in parts:
            reduce(s, p, 0)
            reduce(s, p, 1)

    def d_hidden_of(tokens):
        total = jnp.dot(
            columns(tokens, z * height, height), g["sh"], preferred_element_type=jnp.float32
        )
        for t in range(1, n):
            piece, place = g[f"R{t}E"], jnp.where(z % 2 == 0, z + t, z - t)
            if f"R{n - t}O" in g.rules:
                piece = jnp.where((place >= 0) & (place < n), piece, g[f"R{n - t}O"])
            total = total + jnp.dot(
                columns(tokens, place % n * height, height),
                piece,
                preferred_element_type=jnp.float32,
            )
        return (total * multiplier).astype(jnp.bfloat16)

    def other_tokens():
        a, b = g["o1"], g["o2"]
        return jnp.where(
            near_start == 0, jnp.concatenate([a, b], axis=1), jnp.concatenate([b, a], axis=1)
        )

    g.rule("b", other_tokens, d_hidden_of)
    g.rule("by", lambda: g["b"], over("y"))
    g.rule("me", lambda: g["g"], d_hidden_of)

    def gate_and_up(operands):
        gate, up = (v.astype(jnp.float32) for v in operands)
        d_hidden = in_order(g["me"], g["by"], 1).astype(jnp.float32)
        s = jax.nn.sigmoid(gate)
        d_gate = (d_hidden * up * s * (1.0 + gate * (1.0 - s))).astype(jnp.bfloat16)
        return d_gate, (d_hidden * gate * s).astype(jnp.bfloat16)

    g.rule("out", lambda: lax.optimization_barrier((gate_pre, up_pre, g["h"]))[:2], gate_and_up)

    def total(p):
        def work(even):
            whole = chunk(p, z, n).astype(jnp.float32) + even.astype(jnp.float32)
            return whole + g[f"T{n - 1}O{p}"].astype(jnp.float32)

        g.rule("z" + p, lambda: g[f"T{n - 1}E{p}"], work)

        def rows_of(whose):
            low = g["z" + p].astype(jnp.bfloat16)
            return lax.dynamic_slice_in_dim(low, whose * rows, rows, 0)

        g.rule("e" + p, lambda: rows_of(1 - y), same)
        g.rule("f" + p, lambda: g["e" + p], over("y"))
        g.rule("k" + p, lambda: rows_of(y), same)

    for p in parts:
        total(p)

    grad_square = sum(jnp.sum(g["z" + p] * g["z" + p], axis=1) for p in parts)
    keep = lax.dynamic_slice_in_dim(grad_square, y * rows, rows, 0)
    give = lax.dynamic_slice_in_dim(grad_square, (1 - y) * rows, rows, 0)
    grad_square = keep + lax.ppermute(give, "y", SWAP)
    grad_square = lax.optimization_barrier((grad_square, g["fb"]))[0]
    squares = plane_sum(jnp.stack([g["w2"], grad_square]))
    factor = jnp.minimum(1.0, 0.1 * jnp.sqrt(squares[0]) / jnp.sqrt(squares[1] + 1e-06))
    grad = in_order(
        jnp.concatenate([g["k" + p] for p in parts], 1),
        jnp.concatenate([g["f" + p] for p in parts], 1),
        1,
    ).astype(jnp.float32)
    momentum_new = 0.9 * momentum + grad * factor[:, None]
    w_new = w_down - 0.05 * momentum_new
    d_gate, d_up = g["out"]
    return (d_gate, d_up, w_new, momentum_new)


def solution(mesh):
    groups, parts = mesh.devices.shape
    fine = Mesh(mesh.devices.reshape(groups // 2, 2, parts // 2, 2), ("z", "y", "x", "c"))
    dp, tensor = ("z", "y"), ("x", "c")
    placed = P(dp, tensor)
    return jax.shard_map(
        body,
        mesh=fine,
        in_specs=(P(dp + tensor, None), placed, placed, placed, placed),
        out_specs=(placed,) * 4,
        check_vma=False,
    )
```

```python
import jax
import jax.numpy as jnp
from jax import lax
from jax.sharding import Mesh, PartitionSpec as P

FF = 7168
SWAP = [(0, 1), (1, 0)]
ORDER = {
    "ow": ["gw"],
    "x": ["gw"],
    "h": ["ow"],
    "d1": ["gw"],
    "sa": ["y1", "sh"],
    "d2": ["ta"],
    "sb": ["y2", "S1Ea"],
    "G2E": ["S1Ea", "G2O"],
    "G2O": ["S1Ea"],
    "mb": ["G2E"],
    "S1Eb": ["S2Oa"],
    "S2Ea": ["S1Ea"],
    "S2Oa": ["S2Ea"],
    "G3E": ["S1Eb"],
    "S2Ob": ["S3Ea", "T3Oa"],
    "S3Ea": ["S3Oa", "w2"],
    "S3Oa": ["G3E"],
    "S3Eb": ["b", "S2Ob"],
    "S3Ob": ["S3Eb"],
    "za": ["S3Ob"],
    "zb": ["by"],
    "w2": ["ta"],
    "q2": ["S1Ea"],
    "o2": ["S1Ea"],
    "q1": ["sh"],
    "o1": ["sh"],
    "G1O": ["G1E"],
}
EDGE = "EO"


def plane_sum(value):
    k = lax.axis_size("x") * 2
    across = [(i, k - 1 - i) for i in range(k)]
    return (
        value
        + lax.ppermute(value, "x", SWAP)
        + lax.ppermute(value, "c", SWAP)
        + lax.ppermute(value, ("x", "c"), across)
    )


def edges(n, parity, upward, downward):
    pairs = [(i, i + 1) for i in upward if i % 2 == parity]
    return pairs + [(i, i - 1) for i in downward if (i - 1) % 2 == parity]


class Graph:
    def __init__(self):
        self.rules, self.values, self.open = {}, {}, set()

    def rule(self, name, operand, work):
        self.rules[name] = (operand, work)

    def __getitem__(self, name):
        if name in self.values:
            return self.values[name]
        if name in self.open:
            raise ValueError(name)
        self.open.add(name)
        operand, work = self.rules[name]
        first = operand()
        waits = [self[other] for other in ORDER.get(name, ()) if other in self.rules]
        if waits:
            first = lax.optimization_barrier((first, waits))[0]
        self.values[name] = work(first)
        return self.values[name]


def body(d_out, gate_pre, up_pre, w_down, momentum):
    multiplier = FF ** (-0.5)
    n = lax.axis_size("z")
    z, y, x, c = (lax.axis_index(a) for a in ("z", "y", "x", "c"))
    rows = w_down.shape[0]
    height = 2 * rows
    cols = w_down.shape[1] // 2
    first = -(-cols // 256) * 128
    parts = {"a": (0, first), "b": (first, cols - first)}
    block, depth = d_out.shape
    half = n // 2 * height
    near_start = jnp.where(z < n // 2, depth - half, 0)
    starts = {"1": near_start, "2": depth - half - near_start}
    g = Graph()

    def in_order(a, b, axis):
        return jnp.where(
            y == 0, jnp.concatenate([a, b], axis=axis), jnp.concatenate([b, a], axis=axis)
        )

    def columns(a, start, width):
        return lax.dynamic_slice_in_dim(a, start, width, 1)

    def over(axis):
        return lambda value: lax.ppermute(value, axis, SWAP)

    def same(value):
        return value

    def weights(whose):
        return lambda w: columns(w, whose * cols, cols).astype(jnp.bfloat16)

    g.rule("gw", lambda: w_down, weights(1 - y))
    g.rule("ow", lambda: w_down, weights(y))
    g.rule("pw", lambda: g["gw"], over("y"))
    g.rule("sh", lambda: in_order(g["ow"], g["pw"], 0), same)
    g.rule("w2", lambda: w_down, lambda w: jnp.sum(w * w, axis=1))

    def gather_pairs(s, parity):
        return edges(n, parity, range(s - 1, n - 1), range(1, n - s + 1))

    def gather(s, parity):
        pairs = gather_pairs(s, parity)
        if not pairs:
            return
        name, got = [f"{kind}{s}{EDGE[parity]}" for kind in "GR"]
        other = f"R{s - 1}{EDGE[1 - parity]}"
        g.rule(name, (lambda: g["sh"]) if s == 1 else (lambda: g[other]), same)
        g.rule(got, lambda: g[name], lambda v: lax.ppermute(v, "z", pairs))

    for s in range(1, n):
        gather(s, 0)
        gather(s, 1)

    def hidden(operands):
        gate, up = (v.astype(jnp.float32) for v in operands)
        return (gate * jax.nn.sigmoid(gate) * up).astype(jnp.bfloat16)

    g.rule("h", lambda: (gate_pre, up_pre), hidden)

    def hidden_part(p):
        start, width = parts[p]
        g.rule("m" + p, lambda: columns(g["h"], y * cols + start, width), same)
        g.rule("s" + p, lambda: columns(g["h"], (1 - y) * cols + start, width), same)
        g.rule("t" + p, lambda: g["s" + p], over("y"))

    hidden_part("a")
    hidden_part("b")

    def arrange(operands):
        pair = jnp.concatenate(operands, axis=0)
        other = lax.ppermute(pair, "c", SWAP)
        out = jnp.zeros((4 * block, pair.shape[1]), pair.dtype)
        for source, core in ((pair, c), (other, 1 - c)):
            for k, chip in ((0, x), (1, 1 - x)):
                piece = source[k * block : (k + 1) * block]
                out = lax.dynamic_update_slice_in_dim(out, piece, (chip * 2 + core) * block, 0)
        return out

    g.rule("x", lambda: d_out, over("x"))
    g.rule("g", lambda: (d_out, g["x"]), arrange)

    def cotangents(k):
        g.rule("d" + k, lambda: columns(d_out, starts[k], half), same)
        g.rule("y" + k, lambda: g["d" + k], over("y"))
        g.rule("q" + k, lambda: g["y" + k], over("x"))
        g.rule("o" + k, lambda: (g["y" + k], g["q" + k]), arrange)

    cotangents("1")
    cotangents("2")

    contract = (((0,), (0,)), ((), ()))

    def product(k, p):
        def work(mine):
            partial = lax.dot_general(
                columns(g["g"], starts[k], half),
                mine,
                contract,
                preferred_element_type=jnp.float32,
            ) + lax.dot_general(
                g["o" + k],
                g["t" + p],
                contract,
                preferred_element_type=jnp.float32,
            )
            return (partial * multiplier).astype(jnp.bfloat16)

        g.rule("p" + k + p, lambda: g["m" + p], work)

    for k in starts:
        for p in parts:
            product(k, p)

    def chunk(p, k, s):
        k = jnp.clip(k, 0, n - 1) * height
        at = jnp.clip(k - starts["1"], 0, half - height)
        a = lax.dynamic_slice_in_dim(g["p1" + p], at, height, 0)
        if s <= n // 2:
            return a
        at = jnp.clip(k - starts["2"], 0, half - height)
        b = lax.dynamic_slice_in_dim(g["p2" + p], at, height, 0)
        return jnp.where((k >= starts["1"]) & (k < starts["1"] + half), a, b)

    def reduce(s, p, parity):
        pairs = edges(n, parity, range(0, s), range(n - s, n))
        if not pairs:
            return
        name, before = f"{s}{EDGE[parity]}{p}", f"T{s - 1}{EDGE[1 - parity]}{p}"

        def operand():
            value = chunk(p, jnp.where(z % 2 == parity, n - s + z, s - n + z), s)
            if before not in g.rules:
                return value
            got = g[before]
            return (value.astype(jnp.float32) + got.astype(jnp.float32)).astype(value.dtype)

        g.rule("S" + name, operand, same)
        g.rule("T" + name, lambda: g["S" + name], lambda v: lax.ppermute(v, "z", pairs))

    def first_two(p):
        pairs = edges(n, 0, range(0, 1), range(n - 1, n))
        at = jnp.where(z % 2 == 0, (n - 2) * height, 0) - starts["1"]

        def operand():
            at_most = jnp.clip(at, 0, half - 2 * height)
            return lax.dynamic_slice_in_dim(g["p1" + p], at_most, 2 * height, 0)

        g.rule("S1E" + p, operand, same)
        g.rule("U" + p, lambda: g["S1E" + p], lambda v: lax.ppermute(v, "z", pairs))
        for s, start in ((1, z % 2 * height), (2, (1 - z % 2) * height)):
            g.rule(f"T{s}E{p}", part_of("U" + p, start), same)

    def part_of(name, start):
        return lambda: lax.dynamic_slice_in_dim(g[name], start, height, 0)

    for s in range(1, n):
        for p in parts:
            if p == "a" or s > 2:
                reduce(s, p, 0)
            elif s == 1:
                first_two(p)
            reduce(s, p, 1)

    def d_hidden_of(tokens):
        total = jnp.dot(
            columns(tokens, z * height, height), g["sh"], preferred_element_type=jnp.float32
        )
        for t in range(1, n):
            piece, place = g[f"R{t}E"], jnp.where(z % 2 == 0, z + t, z - t)
            if f"R{n - t}O" in g.rules:
                piece = jnp.where((place >= 0) & (place < n), piece, g[f"R{n - t}O"])
            total = total + jnp.dot(
                columns(tokens, place % n * height, height),
                piece,
                preferred_element_type=jnp.float32,
            )
        return (total * multiplier).astype(jnp.bfloat16)

    def other_tokens():
        a, b = g["o1"], g["o2"]
        return jnp.where(
            near_start == 0, jnp.concatenate([a, b], axis=1), jnp.concatenate([b, a], axis=1)
        )

    g.rule("b", other_tokens, d_hidden_of)
    g.rule("by", lambda: g["b"], over("y"))
    g.rule("me", lambda: g["g"], d_hidden_of)

    def gate_and_up(operands):
        gate, up = (v.astype(jnp.float32) for v in operands)
        d_hidden = in_order(g["me"], g["by"], 1).astype(jnp.float32)
        s = jax.nn.sigmoid(gate)
        d_gate = (d_hidden * up * s * (1.0 + gate * (1.0 - s))).astype(jnp.bfloat16)
        return d_gate, (d_hidden * gate * s).astype(jnp.bfloat16)

    g.rule("out", lambda: lax.optimization_barrier((gate_pre, up_pre, g["h"]))[:2], gate_and_up)

    def total(p):
        def work(even):
            whole = chunk(p, z, n).astype(jnp.float32) + even.astype(jnp.float32)
            return whole + g[f"T{n - 1}O{p}"].astype(jnp.float32)

        g.rule("z" + p, lambda: g[f"T{n - 1}E{p}"], work)

        def rows_of(whose):
            low = g["z" + p].astype(jnp.bfloat16)
            return lax.dynamic_slice_in_dim(low, whose * rows, rows, 0)

        g.rule("e" + p, lambda: rows_of(1 - y), same)
        g.rule("f" + p, lambda: g["e" + p], over("y"))
        g.rule("k" + p, lambda: rows_of(y), same)

    for p in parts:
        total(p)

    def square_sum(name):
        value = g[name].astype(jnp.float32)
        return jnp.sum(value * value, axis=1)

    grad_square = sum(square_sum(kind + p) for p in parts for kind in "kf")
    squares = plane_sum(jnp.stack([g["w2"], grad_square]))
    factor = jnp.minimum(1.0, 0.1 * jnp.sqrt(squares[0]) / jnp.sqrt(squares[1] + 1e-06))
    grad = in_order(
        jnp.concatenate([g["k" + p] for p in parts], 1),
        jnp.concatenate([g["f" + p] for p in parts], 1),
        1,
    ).astype(jnp.float32)
    momentum_new = 0.9 * momentum + grad * factor[:, None]
    w_new = w_down - 0.05 * momentum_new
    d_gate, d_up = g["out"]
    return (d_gate, d_up, w_new, momentum_new)


def solution(mesh):
    groups, parts = mesh.devices.shape
    fine = Mesh(mesh.devices.reshape(groups // 2, 2, parts // 2, 2), ("z", "y", "x", "c"))
    dp, tensor = ("z", "y"), ("x", "c")
    placed = P(dp, tensor)
    return jax.shard_map(
        body,
        mesh=fine,
        in_specs=(P(dp + tensor, None), placed, placed, placed, placed),
        out_specs=(placed,) * 4,
        check_vma=False,
    )
```

```python
import jax
import jax.numpy as jnp
from jax import lax
from jax.sharding import Mesh, PartitionSpec as P

FF = 7168
SWAP = [(0, 1), (1, 0)]
ORDER = {
    "ow": ["gw"],
    "x": ["gw"],
    "h": ["ow"],
    "d1": ["h"],
    "sa": ["y1", "sh"],
    "d2": ["ta"],
    "sb": ["y2", "S1Ea"],
    "G2E": ["S1Ea", "G2O"],
    "G2O": ["S1Ea"],
    "mb": ["G2E"],
    "S1Eb": ["S2Oa"],
    "S2Ea": ["S1Ea"],
    "S2Oa": ["S2Ea"],
    "G3E": ["S1Eb"],
    "S2Ob": ["S3Ea", "T3Oa"],
    "S3Ea": ["S3Oa", "w2"],
    "S3Oa": ["G3E"],
    "S3Eb": ["b", "S2Ob"],
    "S3Ob": ["S3Eb"],
    "za": ["S3Ob"],
    "zb": ["by"],
    "w2": ["ta"],
    "q2": ["S1Ea"],
    "o2": ["S1Ea"],
    "q1": ["sh"],
    "o1": ["sh"],
    "G1O": ["G1E"],
}
EDGE = "EO"


def plane_sum(value):
    k = lax.axis_size("x") * 2
    across = [(i, k - 1 - i) for i in range(k)]
    return (
        value
        + lax.ppermute(value, "x", SWAP)
        + lax.ppermute(value, "c", SWAP)
        + lax.ppermute(value, ("x", "c"), across)
    )


def edges(n, parity, upward, downward):
    pairs = [(i, i + 1) for i in upward if i % 2 == parity]
    return pairs + [(i, i - 1) for i in downward if (i - 1) % 2 == parity]


class Graph:
    def __init__(self):
        self.rules, self.values, self.open = {}, {}, set()

    def rule(self, name, operand, work):
        self.rules[name] = (operand, work)

    def __getitem__(self, name):
        if name in self.values:
            return self.values[name]
        if name in self.open:
            raise ValueError(name)
        self.open.add(name)
        operand, work = self.rules[name]
        first = operand()
        waits = [self[other] for other in ORDER.get(name, ()) if other in self.rules]
        if waits:
            first = lax.optimization_barrier((first, waits))[0]
        self.values[name] = work(first)
        return self.values[name]


def body(d_out, gate_pre, up_pre, w_down, momentum):
    multiplier = FF ** (-0.5)
    n = lax.axis_size("z")
    z, y, x, c = (lax.axis_index(a) for a in ("z", "y", "x", "c"))
    rows = w_down.shape[0]
    height = 2 * rows
    cols = w_down.shape[1] // 2
    first = -(-cols // 256) * 128
    parts = {"a": (0, first), "b": (first, cols - first)}
    block, depth = d_out.shape
    half = n // 2 * height
    near_start = jnp.where(z < n // 2, depth - half, 0)
    starts = {"1": near_start, "2": depth - half - near_start}
    g = Graph()

    def in_order(a, b, axis):
        return jnp.where(
            y == 0, jnp.concatenate([a, b], axis=axis), jnp.concatenate([b, a], axis=axis)
        )

    def columns(a, start, width):
        return lax.dynamic_slice_in_dim(a, start, width, 1)

    def over(axis):
        return lambda value: lax.ppermute(value, axis, SWAP)

    def same(value):
        return value

    def weights(whose):
        return lambda w: columns(w, whose * cols, cols).astype(jnp.bfloat16)

    g.rule("gw", lambda: w_down, weights(1 - y))
    g.rule("ow", lambda: w_down, weights(y))
    g.rule("pw", lambda: g["gw"], over("y"))
    g.rule("sh", lambda: in_order(g["ow"], g["pw"], 0), same)
    g.rule("w2", lambda: w_down, lambda w: jnp.sum(w * w, axis=1))

    def gather_pairs(s, parity):
        return edges(n, parity, range(s - 1, n - 1), range(1, n - s + 1))

    def gather(s, parity):
        pairs = gather_pairs(s, parity)
        if not pairs:
            return
        name, got = [f"{kind}{s}{EDGE[parity]}" for kind in "GR"]
        other = f"R{s - 1}{EDGE[1 - parity]}"
        g.rule(name, (lambda: g["sh"]) if s == 1 else (lambda: g[other]), same)
        g.rule(got, lambda: g[name], lambda v: lax.ppermute(v, "z", pairs))

    for s in range(1, n):
        gather(s, 0)
        gather(s, 1)

    def hidden(operands):
        gate, up = (v.astype(jnp.float32) for v in operands)
        return (gate * jax.nn.sigmoid(gate) * up).astype(jnp.bfloat16)

    g.rule("h", lambda: (gate_pre, up_pre), hidden)

    def hidden_part(p):
        start, width = parts[p]
        g.rule("m" + p, lambda: columns(g["h"], y * cols + start, width), same)
        g.rule("s" + p, lambda: columns(g["h"], (1 - y) * cols + start, width), same)
        g.rule("t" + p, lambda: g["s" + p], over("y"))

    hidden_part("a")
    hidden_part("b")

    def arrange(operands):
        pair = jnp.concatenate(operands, axis=0)
        other = lax.ppermute(pair, "c", SWAP)
        out = jnp.zeros((4 * block, pair.shape[1]), pair.dtype)
        for source, core in ((pair, c), (other, 1 - c)):
            for k, chip in ((0, x), (1, 1 - x)):
                piece = source[k * block : (k + 1) * block]
                out = lax.dynamic_update_slice_in_dim(out, piece, (chip * 2 + core) * block, 0)
        return out

    g.rule("x", lambda: d_out, over("x"))
    g.rule("g", lambda: (d_out, g["x"]), arrange)

    def cotangents(k):
        g.rule("d" + k, lambda: columns(d_out, starts[k], half), same)
        g.rule("y" + k, lambda: g["d" + k], over("y"))
        g.rule("q" + k, lambda: g["y" + k], over("x"))
        g.rule("o" + k, lambda: (g["y" + k], g["q" + k]), arrange)

    cotangents("1")
    cotangents("2")

    contract = (((0,), (0,)), ((), ()))

    def product(k, p):
        def work(mine):
            partial = lax.dot_general(
                columns(g["g"], starts[k], half),
                mine,
                contract,
                preferred_element_type=jnp.float32,
            ) + lax.dot_general(
                g["o" + k],
                g["t" + p],
                contract,
                preferred_element_type=jnp.float32,
            )
            return (partial * multiplier).astype(jnp.bfloat16)

        g.rule("p" + k + p, lambda: g["m" + p], work)

    for k in starts:
        for p in parts:
            product(k, p)

    def chunk(p, k, s):
        k = jnp.clip(k, 0, n - 1) * height
        at = jnp.clip(k - starts["1"], 0, half - height)
        a = lax.dynamic_slice_in_dim(g["p1" + p], at, height, 0)
        if s <= n // 2:
            return a
        at = jnp.clip(k - starts["2"], 0, half - height)
        b = lax.dynamic_slice_in_dim(g["p2" + p], at, height, 0)
        return jnp.where((k >= starts["1"]) & (k < starts["1"] + half), a, b)

    def reduce(s, p, parity):
        pairs = edges(n, parity, range(0, s), range(n - s, n))
        if not pairs:
            return
        name, before = f"{s}{EDGE[parity]}{p}", f"T{s - 1}{EDGE[1 - parity]}{p}"

        def operand():
            value = chunk(p, jnp.where(z % 2 == parity, n - s + z, s - n + z), s)
            if before not in g.rules:
                return value
            got = g[before]
            return (value.astype(jnp.float32) + got.astype(jnp.float32)).astype(value.dtype)

        g.rule("S" + name, operand, same)
        g.rule("T" + name, lambda: g["S" + name], lambda v: lax.ppermute(v, "z", pairs))

    def first_two(p):
        pairs = edges(n, 0, range(0, 1), range(n - 1, n))
        at = jnp.where(z % 2 == 0, (n - 2) * height, 0) - starts["1"]

        def operand():
            at_most = jnp.clip(at, 0, half - 2 * height)
            return lax.dynamic_slice_in_dim(g["p1" + p], at_most, 2 * height, 0)

        g.rule("S1E" + p, operand, same)
        g.rule("U" + p, lambda: g["S1E" + p], lambda v: lax.ppermute(v, "z", pairs))
        for s, start in ((1, z % 2 * height), (2, (1 - z % 2) * height)):
            g.rule(f"T{s}E{p}", part_of("U" + p, start), same)

    def part_of(name, start):
        return lambda: lax.dynamic_slice_in_dim(g[name], start, height, 0)

    for s in range(1, n):
        for p in parts:
            if p == "a" or s > 2:
                reduce(s, p, 0)
            elif s == 1:
                first_two(p)
            reduce(s, p, 1)

    def d_hidden_of(tokens):
        total = jnp.dot(
            columns(tokens, z * height, height), g["sh"], preferred_element_type=jnp.float32
        )
        for t in range(1, n):
            piece, place = g[f"R{t}E"], jnp.where(z % 2 == 0, z + t, z - t)
            if f"R{n - t}O" in g.rules:
                piece = jnp.where((place >= 0) & (place < n), piece, g[f"R{n - t}O"])
            total = total + jnp.dot(
                columns(tokens, place % n * height, height),
                piece,
                preferred_element_type=jnp.float32,
            )
        return (total * multiplier).astype(jnp.bfloat16)

    def other_tokens():
        a, b = g["o1"], g["o2"]
        return jnp.where(
            near_start == 0, jnp.concatenate([a, b], axis=1), jnp.concatenate([b, a], axis=1)
        )

    g.rule("b", other_tokens, d_hidden_of)
    g.rule("by", lambda: g["b"], over("y"))
    g.rule("me", lambda: g["g"], d_hidden_of)

    def gate_and_up(operands):
        gate, up = (v.astype(jnp.float32) for v in operands)
        d_hidden = in_order(g["me"], g["by"], 1).astype(jnp.float32)
        s = jax.nn.sigmoid(gate)
        d_gate = (d_hidden * up * s * (1.0 + gate * (1.0 - s))).astype(jnp.bfloat16)
        return d_gate, (d_hidden * gate * s).astype(jnp.bfloat16)

    g.rule("out", lambda: lax.optimization_barrier((gate_pre, up_pre, g["h"]))[:2], gate_and_up)

    def total(p):
        def work(even):
            whole = chunk(p, z, n).astype(jnp.float32) + even.astype(jnp.float32)
            return whole + g[f"T{n - 1}O{p}"].astype(jnp.float32)

        g.rule("z" + p, lambda: g[f"T{n - 1}E{p}"], work)

        def rows_of(whose):
            low = g["z" + p].astype(jnp.bfloat16)
            return lax.dynamic_slice_in_dim(low, whose * rows, rows, 0)

        g.rule("e" + p, lambda: rows_of(1 - y), same)
        g.rule("f" + p, lambda: g["e" + p], over("y"))
        g.rule("k" + p, lambda: rows_of(y), same)

    for p in parts:
        total(p)

    def square_sum(name):
        value = g[name].astype(jnp.float32)
        return jnp.sum(value * value, axis=1)

    grad_square = sum(square_sum(kind + p) for p in parts for kind in "kf")
    squares = plane_sum(jnp.stack([g["w2"], grad_square]))
    factor = jnp.minimum(1.0, 0.1 * jnp.sqrt(squares[0]) / jnp.sqrt(squares[1] + 1e-06))
    grad = in_order(
        jnp.concatenate([g["k" + p] for p in parts], 1),
        jnp.concatenate([g["f" + p] for p in parts], 1),
        1,
    ).astype(jnp.float32)
    momentum_new = 0.9 * momentum + grad * factor[:, None]
    w_new = w_down - 0.05 * momentum_new
    d_gate, d_up = g["out"]
    return (d_gate, d_up, w_new, momentum_new)


def solution(mesh):
    groups, parts = mesh.devices.shape
    fine = Mesh(mesh.devices.reshape(groups // 2, 2, parts // 2, 2), ("z", "y", "x", "c"))
    dp, tensor = ("z", "y"), ("x", "c")
    placed = P(dp, tensor)
    return jax.shard_map(
        body,
        mesh=fine,
        in_specs=(P(dp + tensor, None), placed, placed, placed, placed),
        out_specs=(placed,) * 4,
        check_vma=False,
    )
```

```python
import jax
import jax.numpy as jnp
from jax import lax
from jax.sharding import Mesh, PartitionSpec as P

FF = 7168
SWAP = [(0, 1), (1, 0)]
ORDER = {
    "ow": ["gw"],
    "x": ["gw"],
    "h": ["ow"],
    "d1": ["h"],
    "sa": ["y1", "sh"],
    "d2": ["ta"],
    "sb": ["y2", "S1Ea"],
    "G2E": ["S1Ea", "G2O"],
    "G2O": ["S1Ea"],
    "mb": ["G2E"],
    "S1Eb": ["S2Oa"],
    "S2Ea": ["S1Ea"],
    "S2Oa": ["S2Ea"],
    "G3E": ["S1Eb"],
    "S2Ob": ["S3Ea", "T3Oa"],
    "S3Ea": ["S3Oa", "w2"],
    "S3Oa": ["G3E"],
    "S3Eb": ["b", "S2Ob"],
    "S3Ob": ["S3Eb"],
    "za": ["S3Ob"],
    "zb": ["by"],
    "w2": ["ta"],
    "q2": ["S1Ea"],
    "o2": ["S1Ea"],
    "q1": ["sh", "sa"],
    "o1": ["sh"],
    "G1O": ["G1E"],
    "va": ["out", "eb"],
}
EDGE = "EO"


def plane_sum(value):
    k = lax.axis_size("x") * 2
    across = [(i, k - 1 - i) for i in range(k)]
    return (
        value
        + lax.ppermute(value, "x", SWAP)
        + lax.ppermute(value, "c", SWAP)
        + lax.ppermute(value, ("x", "c"), across)
    )


def edges(n, parity, upward, downward):
    pairs = [(i, i + 1) for i in upward if i % 2 == parity]
    return pairs + [(i, i - 1) for i in downward if (i - 1) % 2 == parity]


class Graph:
    def __init__(self):
        self.rules, self.values, self.open = {}, {}, set()

    def rule(self, name, operand, work):
        self.rules[name] = (operand, work)

    def __getitem__(self, name):
        if name in self.values:
            return self.values[name]
        if name in self.open:
            raise ValueError(name)
        self.open.add(name)
        operand, work = self.rules[name]
        first = operand()
        waits = [self[other] for other in ORDER.get(name, ()) if other in self.rules]
        if waits:
            first = lax.optimization_barrier((first, waits))[0]
        self.values[name] = work(first)
        return self.values[name]


def body(d_out, gate_pre, up_pre, w_down, momentum):
    multiplier = FF ** (-0.5)
    n = lax.axis_size("z")
    z, y, x, c = (lax.axis_index(a) for a in ("z", "y", "x", "c"))
    rows = w_down.shape[0]
    height = 2 * rows
    cols = w_down.shape[1] // 2
    first = -(-cols // 256) * 128
    parts = {"a": (0, first), "b": (first, cols - first)}
    block, depth = d_out.shape
    half = n // 2 * height
    near_start = jnp.where(z < n // 2, depth - half, 0)
    starts = {"1": near_start, "2": depth - half - near_start}
    g = Graph()

    def in_order(a, b, axis):
        return jnp.where(
            y == 0, jnp.concatenate([a, b], axis=axis), jnp.concatenate([b, a], axis=axis)
        )

    def columns(a, start, width):
        return lax.dynamic_slice_in_dim(a, start, width, 1)

    def over(axis):
        return lambda value: lax.ppermute(value, axis, SWAP)

    def same(value):
        return value

    def weights(whose):
        return lambda w: columns(w, whose * cols, cols).astype(jnp.bfloat16)

    g.rule("gw", lambda: w_down, weights(1 - y))
    g.rule("ow", lambda: w_down, weights(y))
    g.rule("pw", lambda: g["gw"], over("y"))
    g.rule("sh", lambda: in_order(g["ow"], g["pw"], 0), same)
    g.rule("w2", lambda: w_down, lambda w: jnp.sum(w * w, axis=1))

    def gather_pairs(s, parity):
        return edges(n, parity, range(s - 1, n - 1), range(1, n - s + 1))

    def gather(s, parity):
        pairs = gather_pairs(s, parity)
        if not pairs:
            return
        name, got = [f"{kind}{s}{EDGE[parity]}" for kind in "GR"]
        other = f"R{s - 1}{EDGE[1 - parity]}"
        g.rule(name, (lambda: g["sh"]) if s == 1 else (lambda: g[other]), same)
        g.rule(got, lambda: g[name], lambda v: lax.ppermute(v, "z", pairs))

    for s in range(1, n):
        gather(s, 0)
        gather(s, 1)

    def hidden(operands):
        gate, up = (v.astype(jnp.float32) for v in operands)
        return (gate * jax.nn.sigmoid(gate) * up).astype(jnp.bfloat16)

    g.rule("h", lambda: (gate_pre, up_pre), hidden)

    def hidden_part(p):
        start, width = parts[p]
        g.rule("m" + p, lambda: columns(g["h"], y * cols + start, width), same)
        g.rule("s" + p, lambda: columns(g["h"], (1 - y) * cols + start, width), same)
        g.rule("t" + p, lambda: g["s" + p], over("y"))

    hidden_part("a")
    hidden_part("b")

    def arrange(operands):
        pair = jnp.concatenate(operands, axis=0)
        other = lax.ppermute(pair, "c", SWAP)
        out = jnp.zeros((4 * block, pair.shape[1]), pair.dtype)
        for source, core in ((pair, c), (other, 1 - c)):
            for k, chip in ((0, x), (1, 1 - x)):
                piece = source[k * block : (k + 1) * block]
                out = lax.dynamic_update_slice_in_dim(out, piece, (chip * 2 + core) * block, 0)
        return out

    g.rule("x", lambda: d_out, over("x"))
    g.rule("g", lambda: (d_out, g["x"]), arrange)

    def cotangents(k):
        g.rule("d" + k, lambda: columns(d_out, starts[k], half), same)
        g.rule("y" + k, lambda: g["d" + k], over("y"))
        g.rule("q" + k, lambda: g["y" + k], over("x"))
        g.rule("o" + k, lambda: (g["y" + k], g["q" + k]), arrange)

    cotangents("1")
    cotangents("2")

    contract = (((0,), (0,)), ((), ()))

    def product(k, p):
        def work(mine):
            partial = lax.dot_general(
                columns(g["g"], starts[k], half),
                mine,
                contract,
                preferred_element_type=jnp.float32,
            ) + lax.dot_general(
                g["o" + k],
                g["t" + p],
                contract,
                preferred_element_type=jnp.float32,
            )
            return (partial * multiplier).astype(jnp.bfloat16)

        g.rule("p" + k + p, lambda: g["m" + p], work)

    for k in starts:
        for p in parts:
            product(k, p)

    def chunk(p, k, s):
        k = jnp.clip(k, 0, n - 1) * height
        at = jnp.clip(k - starts["1"], 0, half - height)
        a = lax.dynamic_slice_in_dim(g["p1" + p], at, height, 0)
        if s <= n // 2:
            return a
        at = jnp.clip(k - starts["2"], 0, half - height)
        b = lax.dynamic_slice_in_dim(g["p2" + p], at, height, 0)
        return jnp.where((k >= starts["1"]) & (k < starts["1"] + half), a, b)

    def reduce(s, p, parity):
        pairs = edges(n, parity, range(0, s), range(n - s, n))
        if not pairs:
            return
        name, before = f"{s}{EDGE[parity]}{p}", f"T{s - 1}{EDGE[1 - parity]}{p}"

        def operand():
            value = chunk(p, jnp.where(z % 2 == parity, n - s + z, s - n + z), s)
            if before not in g.rules:
                return value
            got = g[before]
            return (value.astype(jnp.float32) + got.astype(jnp.float32)).astype(value.dtype)

        g.rule("S" + name, operand, same)
        g.rule("T" + name, lambda: g["S" + name], lambda v: lax.ppermute(v, "z", pairs))

    def first_two(p):
        pairs = edges(n, 0, range(0, 1), range(n - 1, n))
        at = jnp.where(z % 2 == 0, (n - 2) * height, 0) - starts["1"]

        def operand():
            at_most = jnp.clip(at, 0, half - 2 * height)
            return lax.dynamic_slice_in_dim(g["p1" + p], at_most, 2 * height, 0)

        g.rule("S1E" + p, operand, same)
        g.rule("U" + p, lambda: g["S1E" + p], lambda v: lax.ppermute(v, "z", pairs))
        for s, start in ((1, z % 2 * height), (2, (1 - z % 2) * height)):
            g.rule(f"T{s}E{p}", part_of("U" + p, start), same)

    def part_of(name, start):
        return lambda: lax.dynamic_slice_in_dim(g[name], start, height, 0)

    for s in range(1, n):
        for p in parts:
            if p == "a" or s > 2:
                reduce(s, p, 0)
            elif s == 1:
                first_two(p)
            reduce(s, p, 1)

    def d_hidden_of(tokens):
        total = jnp.dot(
            columns(tokens, z * height, height), g["sh"], preferred_element_type=jnp.float32
        )
        for t in range(1, n):
            piece, place = g[f"R{t}E"], jnp.where(z % 2 == 0, z + t, z - t)
            if f"R{n - t}O" in g.rules:
                piece = jnp.where((place >= 0) & (place < n), piece, g[f"R{n - t}O"])
            total = total + jnp.dot(
                columns(tokens, place % n * height, height),
                piece,
                preferred_element_type=jnp.float32,
            )
        return (total * multiplier).astype(jnp.bfloat16)

    def other_tokens():
        a, b = g["o1"], g["o2"]
        return jnp.where(
            near_start == 0, jnp.concatenate([a, b], axis=1), jnp.concatenate([b, a], axis=1)
        )

    g.rule("b", other_tokens, d_hidden_of)
    g.rule("by", lambda: g["b"], over("y"))
    g.rule("me", lambda: g["g"], d_hidden_of)

    def gate_and_up(operands):
        gate, up = (v.astype(jnp.float32) for v in operands)
        d_hidden = in_order(g["me"], g["by"], 1).astype(jnp.float32)
        s = jax.nn.sigmoid(gate)
        d_gate = (d_hidden * up * s * (1.0 + gate * (1.0 - s))).astype(jnp.bfloat16)
        return d_gate, (d_hidden * gate * s).astype(jnp.bfloat16)

    g.rule("out", lambda: lax.optimization_barrier((gate_pre, up_pre, g["h"]))[:2], gate_and_up)

    def total(p):
        def work(even):
            whole = chunk(p, z, n).astype(jnp.float32) + even.astype(jnp.float32)
            return whole + g[f"T{n - 1}O{p}"].astype(jnp.float32)

        g.rule("z" + p, lambda: g[f"T{n - 1}E{p}"], work)

        def rows_of(whose):
            low = g["z" + p].astype(jnp.bfloat16)
            return lax.dynamic_slice_in_dim(low, whose * rows, rows, 0)

        g.rule("e" + p, lambda: rows_of(1 - y), same)
        g.rule("f" + p, lambda: g["e" + p], over("y"))
        g.rule("k" + p, lambda: rows_of(y), same)
        g.rule("v" + p, lambda: g["f" + p], same)

    for p in parts:
        total(p)

    def square_sum(name):
        value = g[name].astype(jnp.float32)
        return jnp.sum(value * value, axis=1)

    grad_square = sum(square_sum(kind + p) for p in parts for kind in "kv")
    squares = plane_sum(jnp.stack([g["w2"], grad_square]))
    factor = jnp.minimum(1.0, 0.1 * jnp.sqrt(squares[0]) / jnp.sqrt(squares[1] + 1e-06))
    grad = in_order(
        jnp.concatenate([g["k" + p] for p in parts], 1),
        jnp.concatenate([g["v" + p] for p in parts], 1),
        1,
    ).astype(jnp.float32)
    momentum_new = 0.9 * momentum + grad * factor[:, None]
    w_new = w_down - 0.05 * momentum_new
    d_gate, d_up = g["out"]
    return (d_gate, d_up, w_new, momentum_new)


def solution(mesh):
    groups, parts = mesh.devices.shape
    fine = Mesh(mesh.devices.reshape(groups // 2, 2, parts // 2, 2), ("z", "y", "x", "c"))
    dp, tensor = ("z", "y"), ("x", "c")
    placed = P(dp, tensor)
    return jax.shard_map(
        body,
        mesh=fine,
        in_specs=(P(dp + tensor, None), placed, placed, placed, placed),
        out_specs=(placed,) * 4,
        check_vma=False,
    )
```
